32 devices in a mesh: group: 4 (over z), bulk: 8 (over y, x, core).
Axes of the slice: x: 2, y: 2, z: 4, core: 2. Of those that a mesh axis runs over, the one named last changes fastest.
Arguments:
- p_tiles: float32 [1536, 128, 128], P(('group', 'bulk')), may hold values from -0.5 to 0.5
- a_tiles: float32 [1536, 7, 128, 128], P(('group', 'bulk')), may hold values from -0.5 to 0.5
- col_ref: int32 [1536, 7], P(('group', 'bulk')), may hold values from 0 to 111, as said below
- send_list: int32 [32, 2, 32], P(('group', 'bulk')), may hold values from -1 to 47, as said below
- coarse_tile: int32 [1536, 7], P(('group', 'bulk')), may hold values from 0 to 127
Outputs:
- coarse_op: float32 [512, 128, 128], P('group')
The draws below stay inside these ranges and needn't reach their ends.
Inputs may be any that keep to these rules, and one draw needn't show every extreme that they name: `send_list`: entry [s, 0, j] is the local index of a fine block of device s that device s - 1 receives in slot j, entry [s, 1, j] one that device s + 1 receives; the slots of one entry hold distinct blocks, filled slots come first, -1 marks an empty slot. Device 0 sends nothing below and the last device nothing above; every other pair fills between 16 and 32 slots, and device 0 fills all 32 slots for device 1. `col_ref`: on device d, a value v under 48 names d's own fine block v; a value v of 48 or more names the tile that d receives in slot (v - 48) % 32 from the slab below if (v - 48) // 32 is 0, from the slab above if it is 1, always a filled slot. Every filled slot that d receives is named by exactly one coupling of d.
All inputs are finite; a program needn't handle non-finite values.
Results may differ from the reference program's by a relative error of at most 0.0003.
Values sent between devices are 32-bit elements; how exact they have to be, the bound alone decides.
A program may use at most 192 MiB of HBM per device.

```python
import jax
import jax.numpy as jnp
from jax import lax

BS = 128
CW = 128
K = 7
SCAP = 32
FB = 48
CT = 128
PEERS = 32
FINE = 1536
N_GROUP = 4
N_BULK = 8


def routing(key):
    count_key = jax.random.fold_in(key, 101)
    order_key = jax.random.fold_in(key, 102)
    counts = jax.random.randint(count_key, (PEERS, 2), SCAP // 2, SCAP + 1)
    sender = jnp.arange(PEERS)
    counts = counts.at[:, 0].set(jnp.where(sender == 0, 0, counts[:, 0]))
    counts = counts.at[:, 1].set(jnp.where(sender == PEERS - 1, 0, counts[:, 1]))
    counts = counts.at[0, 1].set(SCAP)
    scores = jax.random.randint(order_key, (PEERS, 2, FB), 0, 2 ** 20) * FB + jnp.arange(FB)
    order = jnp.argsort(scores, axis=-1)[:, :, :SCAP]
    slots = jnp.arange(SCAP)[None, None, :]
    sends = jnp.where(slots < counts[:, :, None], order, -1).astype(jnp.int32)
    return (counts, sends)


def draw_send_list(key, part):
    counts, sends = routing(key)
    return sends


def draw_col_ref(key, part):
    counts, sends = routing(key)
    key = jax.random.fold_in(key, 7)
    place_key = jax.random.fold_in(key, 1)
    local_key = jax.random.fold_in(key, 2)
    refs = 2 * SCAP
    places = FB * K
    zero = jnp.zeros((1,), counts.dtype)
    below = jnp.concatenate([zero, counts[:-1, 1]])
    above = jnp.concatenate([counts[1:, 0], zero])
    received = jnp.stack([below, above], axis=1)
    scores = jax.random.randint(place_key, (PEERS, places), 0, 2 ** 20) * places + jnp.arange(places)
    ranking = jnp.argsort(jnp.argsort(scores, axis=-1), axis=-1)
    live_table = (jnp.arange(SCAP)[None, None, :] < received[:, :, None]).reshape(PEERS, refs)
    picked = jnp.take_along_axis(live_table, jnp.minimum(ranking, refs - 1), axis=1)
    usable = (ranking < refs) & picked
    local = jax.random.randint(local_key, (PEERS, places), 0, FB)
    chosen = jnp.where(usable, FB + ranking, local)
    return chosen.reshape(PEERS * FB, K).astype(jnp.int32)


def plant(array, rng, least, high):
    extent = array.shape
    index_at = [jax.random.randint(jax.random.fold_in(rng, axis), (), 0, extent[axis]) for axis in range(len(extent))]
    array = array.at[tuple(index_at)].set(least)
    longest = extent.index(max(extent))
    index_at[longest] = (index_at[longest] + 1) % extent[longest]
    return array.at[tuple(index_at)].set(high)


def level_of(stream_key, dims, shards, smallest, high):
    def one(position, blocks):
        heights = jax.random.uniform(jax.random.fold_in(jax.random.fold_in(stream_key, 6), position), (blocks,), jnp.float32, smallest / len(shards), high / len(shards))
        return jnp.repeat(jnp.exp(heights), dims[position] // blocks).reshape((-1,) + (1,) * (len(dims) - position - 1))

    gain = one(*shards[0])
    for cut in shards[1:]:
        gain = gain * one(*cut)
    return gain


def gaussian(own_key, dims, width, limit, split=(), kind=jnp.bfloat16):
    gain = level_of(own_key, dims, split, -0.22, 0.18) if split else 1.0
    entries = jax.random.normal(own_key, dims, jnp.float32) * width * gain
    return jnp.minimum(jnp.maximum(entries, -limit), limit).astype(kind)


def setup_inputs(seed: int = 0) -> dict:
    key_of = jax.random.split(jax.random.key(seed), 6)
    return {
        "p_tiles": gaussian(key_of[0], (FINE, BS, CW), BS ** -0.5, 0.5, ((0, 32),), jnp.float32),
        "a_tiles": gaussian(key_of[1], (FINE, K, BS, BS), BS ** -0.5, 0.5, ((0, 32),), jnp.float32),
        "col_ref": draw_col_ref(jax.random.fold_in(key_of[5], 71), 0),
        "send_list": draw_send_list(jax.random.fold_in(key_of[5], 71), 0),
        "coarse_tile": plant(jax.random.randint(key_of[4], (FINE, K), 0, CT), jax.random.fold_in(key_of[4], 1), 0, CT - 1).astype(jnp.int32),
    }


def reference(p_tiles, a_tiles, col_ref, send_list, coarse_tile):
    owner = (jnp.arange(PEERS * FB, dtype=jnp.int32) // FB)[:, None]
    owner = jnp.broadcast_to(owner, col_ref.shape)
    remote = col_ref - FB
    side = jnp.clip(remote // SCAP, 0, 1).astype(jnp.int32)
    slot_index = jnp.clip(remote % SCAP, 0, SCAP - 1).astype(jnp.int32)
    source = jnp.clip(owner + 2 * side - 1, 0, PEERS - 1).astype(jnp.int32)
    sent_block = send_list[source, (1 - side).astype(jnp.int32), slot_index]
    global_col = jnp.where(col_ref < FB, owner * FB + col_ref, source * FB + jnp.maximum(sent_block, 0)).astype(jnp.int32)

    def one_device(device):
        start = (device * FB).astype(jnp.int32)
        row_tiles = lax.dynamic_slice_in_dim(p_tiles, start, FB, 0)
        couplings = lax.dynamic_slice_in_dim(a_tiles, start, FB, 0).reshape(FB * K, BS, BS)
        col_index = lax.dynamic_slice_in_dim(global_col, start, FB, 0).reshape(-1)
        targets = lax.dynamic_slice_in_dim(coarse_tile, start, FB, 0).reshape(-1)
        right_tiles = p_tiles[col_index]
        product = jnp.einsum("qxy,qyc->qxc", couplings, right_tiles, precision=lax.Precision.HIGHEST)
        triple = jnp.einsum("ixa,ikxc->ikac", row_tiles, product.reshape(FB, K, BS, CW), precision=lax.Precision.HIGHEST)
        return jax.ops.segment_sum(triple.reshape(FB * K, CW, CW), targets, num_segments=CT)

    def group_sum(group_index):
        def add_slab(running, bulk_index):
            return running + one_device(group_index * N_BULK + bulk_index), None

        running, _ = lax.scan(add_slab, jnp.zeros((CT, CW, CW), jnp.float32), jnp.arange(N_BULK, dtype=jnp.int32))
        return running

    result = lax.map(group_sum, jnp.arange(N_GROUP, dtype=jnp.int32))
    return result.reshape(N_GROUP * CT, CW, CW)
```

```python
import functools

import jax
import jax.numpy as jnp
from jax import lax
from jax.experimental import pallas as pl
from jax.experimental.pallas import tpu as pltpu
from jax.sharding import PartitionSpec as P

CT = 128
STEP_BLOCKS = 4
CHUNKS = 8
VMEM_BYTES = 56 * 1024 * 1024


def shifted(block, axis, distance):
    devices = range(lax.axis_size(axis))
    route = [(i - distance, i) for i in devices if i - distance in devices]
    return lax.ppermute(block, axis, route)


def halves(x):
    high = x.astype(jnp.bfloat16)
    low = (x - high.astype(jnp.float32)).astype(jnp.bfloat16)
    return high, low


def left_form(x):
    return jnp.concatenate(halves(x), axis=1)


def right_form(x):
    row = jnp.concatenate(halves(x), axis=1)
    return jnp.concatenate([row, row], axis=0)


def product(left, right):
    both = jnp.dot(left, right, preferred_element_type=jnp.float32)
    width = both.shape[1] // 2
    return both[:, :width] + both[:, width:]


def pick_kernel(send_ref, p_ref, below_ref, above_ref, sem):
    capacity = send_ref.shape[2]

    def copy(side, j):
        target = below_ref if side == 0 else above_ref
        row = jnp.maximum(send_ref[0, side, j], 0)
        return pltpu.make_async_copy(p_ref.at[row], target.at[j], sem.at[side, j])

    for side in range(2):
        @pl.loop(0, capacity)
        def _(j):
            copy(side, j).start()
    for side in range(2):
        @pl.loop(0, capacity)
        def _(j):
            copy(side, j).wait()


def local_kernel(col_ref, tile_ref, p_ref, a_ref, sum_ref, left_ref, place_ref, right_p):
    blocks = p_ref.shape[0]
    neighbours = a_ref.shape[1]
    slots = left_ref.shape[0] - 1
    step = pl.program_id(0)

    @pl.when(step == 0)
    def _():
        @pl.loop(0, blocks)
        def _(f):
            right_p[f] = right_form(p_ref[f])

        @pl.loop(0, sum_ref.shape[0])
        def _(t):
            sum_ref[t] = jnp.zeros(sum_ref.shape[1:], jnp.float32)

        @pl.loop(0, slots + 1)
        def _(j):
            place_ref[j] = -1

    for i in range(STEP_BLOCKS):
        f = step * STEP_BLOCKS + i
        p_left = left_form(p_ref[f].T)
        for k in range(neighbours):
            v = col_ref[f, k]
            t = tile_ref[f, k]
            local = v < blocks
            slot = jnp.where(local, slots, v - blocks)
            left = product(p_left, right_form(a_ref[i, k]))
            left_cat = left_form(left)
            left_ref[slot] = left_cat
            place_ref[slot] = t
            triple = product(left_cat, right_p[jnp.minimum(v, blocks - 1)])
            sum_ref[t] += jnp.where(local, triple, 0.0)


def halo_kernel(place_ref, partial_ref, left_ref, lower_ref, upper_ref, sum_ref, sem):
    capacity = lower_ref.shape[0]
    load = pltpu.make_async_copy(partial_ref, sum_ref, sem)
    load.start()
    load.wait()
    for side, tiles in enumerate((lower_ref, upper_ref)):
        @pl.loop(0, capacity // 4)
        def _(group):
            for i in range(4):
                j = group * 4 + i
                place = place_ref[side * capacity + j]
                triple = product(left_ref[side * capacity + j], right_form(tiles[j]))
                sum_ref[jnp.maximum(place, 0)] += jnp.where(place >= 0, triple, 0.0)


def reduce_kernel(orders, part_ref, out_ref, mine, *rest):
    stages = len(orders[0])
    bufs = rest[:stages]
    load_sem, send_sem, recv_sem = rest[stages:]
    me = lax.axis_index("bulk")
    tiles = part_ref.shape[0]
    chunks = mine.shape[0]
    width = tiles // chunks
    ways = len(orders)
    bit = [(me // 2**b) % 2 for b in range(stages)]
    partner = [me + 2**b * (1 - 2 * bit[b]) for b in range(stages)]

    def load(c, way):
        first = orders[way][0]
        at = c * width + bit[first] * (width // 2)
        return pltpu.make_async_copy(part_ref.at[pl.ds(at, width // 2)], mine.at[c], load_sem.at[c])

    def keep(c, way, s):
        at = c * width
        size = width
        for level in range(s + 1):
            size //= 2
            at = at + bit[orders[way][level]] * size
        return at, size

    def scatter(c, way, s):
        b = orders[way][s]
        size = width >> (s + 1)
        if s == 0:
            src = part_ref.at[pl.ds(c * width + (1 - bit[b]) * size, size)]
        else:
            src = bufs[s - 1].at[c, pl.ds((1 - bit[b]) * size, size)]
        return pltpu.make_async_remote_copy(
            src_ref=src, dst_ref=bufs[s].at[c], send_sem=send_sem.at[s, c], recv_sem=recv_sem.at[s, c],
            device_id={"bulk": partner[b]}, device_id_type=pl.DeviceIdType.MESH)

    def gather(c, way, s):
        b = orders[way][s]
        at, size = keep(c, way, s)
        region = out_ref.at[pl.ds(at, size)]
        n = 2 * stages - 1 - s
        return pltpu.make_async_remote_copy(
            src_ref=region, dst_ref=region, send_sem=send_sem.at[n, c], recv_sem=recv_sem.at[n, c],
            device_id={"bulk": partner[b]}, device_id_type=pl.DeviceIdType.MESH)

    def add(c, way, s):
        b = orders[way][s]
        size = width >> (s + 1)
        at, _ = keep(c, way, s)

        @pl.loop(0, size)
        def _(j):
            if s == 0:
                own = mine[c, j]
            else:
                own = bufs[s - 1][c, bit[b] * size + j]
            total = bufs[s][c, j] + own
            if s == stages - 1:
                out_ref[at + j] = total
            else:
                bufs[s][c, j] = total

    def each(body):
        @pl.loop(0, chunks // ways)
        def _(g):
            for way in range(ways):
                body(g * ways + way, way)

    each(lambda c, way: load(c, way).start())
    barrier = pltpu.get_barrier_semaphore()
    for b in range(stages):
        pl.semaphore_signal(barrier, inc=1, device_id={"bulk": partner[b]}, device_id_type=pl.DeviceIdType.MESH)
    pl.semaphore_wait(barrier, stages)

    each(lambda c, way: scatter(c, way, 0).start())
    for s in range(stages):
        def reduce_step(c, way, s=s):
            if s == 0:
                load(c, way).wait()
            scatter(c, way, s).wait_recv()
            add(c, way, s)
            if s + 1 < stages:
                scatter(c, way, s + 1).start()
            else:
                gather(c, way, s).start()
        each(reduce_step)
    for s in reversed(range(stages)):
        def spread_step(c, way, s=s):
            gather(c, way, s).wait_recv()
            if s > 0:
                gather(c, way, s - 1).start()
        each(spread_step)

    def drain(c, way):
        for s in range(stages):
            scatter(c, way, s).wait_send()
            gather(c, way, s).wait_send()
    each(drain)


def group_sum(partial):
    devices = lax.axis_size("bulk")
    stages = devices.bit_length() - 1
    tiles, rows, columns = partial.shape
    width = tiles // CHUNKS
    bits = tuple(range(stages))
    if stages % 2:
        half = (stages - 1) // 2
        orders = (bits, bits[:1] + bits[1 + half:] + bits[1:1 + half])
    else:
        orders = (bits, bits[stages // 2:] + bits[:stages // 2])
    tile = (rows, columns)
    vmem = functools.partial(pltpu.VMEM, dtype=jnp.float32)
    return pl.pallas_call(
        functools.partial(reduce_kernel, orders),
        out_shape=jax.ShapeDtypeStruct(partial.shape, jnp.float32),
        in_specs=[pl.BlockSpec(memory_space=pl.ANY)],
        out_specs=pl.BlockSpec(memory_space=pltpu.VMEM),
        scratch_shapes=[vmem((CHUNKS, width // 2) + tile)]
        + [vmem((CHUNKS, width >> (s + 1)) + tile) for s in range(stages)]
        + [
            pltpu.SemaphoreType.DMA((CHUNKS,)),
            pltpu.SemaphoreType.DMA((2 * stages, CHUNKS)),
            pltpu.SemaphoreType.DMA((2 * stages, CHUNKS)),
        ],
        compiler_params=pltpu.CompilerParams(
            collective_id=0, has_side_effects=True, vmem_limit_bytes=VMEM_BYTES),
        cost_estimate=pl.CostEstimate(flops=tiles * rows * columns, bytes_accessed=8 * tiles * rows * columns, transcendentals=0),
        name="group_sum",
    )(partial)


def shards(p_tiles, a_tiles, col_ref, send_list, coarse_tile):
    blocks, rows, columns = p_tiles.shape
    neighbours = a_tiles.shape[1]
    capacity = send_list.shape[2]
    slots = 2 * capacity
    tile = (rows, columns)
    any_spec = pl.BlockSpec(memory_space=pl.ANY)
    smem_spec = pl.BlockSpec(memory_space=pltpu.SMEM)
    vmem_spec = pl.BlockSpec(memory_space=pltpu.VMEM)

    sent = jax.ShapeDtypeStruct((capacity,) + tile, jnp.float32)
    to_below, to_above = pl.pallas_call(
        pick_kernel,
        out_shape=(sent, sent),
        in_specs=[smem_spec, any_spec],
        out_specs=(any_spec, any_spec),
        scratch_shapes=[pltpu.SemaphoreType.DMA((2, capacity))],
        name="pick",
    )(send_list, p_tiles)
    lower = shifted(to_above, ("group", "bulk"), 1)
    upper = shifted(to_below, ("group", "bulk"), -1)

    couplings = blocks * neighbours
    whole = lambda *shape: pl.BlockSpec(shape, lambda s, *_: (0,) * len(shape))
    partial, left, place = pl.pallas_call(
        local_kernel,
        out_shape=(
            jax.ShapeDtypeStruct((CT,) + tile, jnp.float32),
            jax.ShapeDtypeStruct((slots + 1, rows, 2 * columns), jnp.bfloat16),
            jax.ShapeDtypeStruct((slots + 1,), jnp.int32),
        ),
        grid_spec=pltpu.PrefetchScalarGridSpec(
            num_scalar_prefetch=2,
            grid=(blocks // STEP_BLOCKS,),
            in_specs=[
                whole(blocks, *tile),
                pl.BlockSpec((STEP_BLOCKS, neighbours) + tile, lambda s, *_: (s, 0, 0, 0)),
            ],
            out_specs=(whole(CT, *tile), whole(slots + 1, rows, 2 * columns), pl.BlockSpec(memory_space=pltpu.SMEM)),
            scratch_shapes=[pltpu.VMEM((blocks, 2 * rows, 2 * columns), jnp.bfloat16)],
        ),
        compiler_params=pltpu.CompilerParams(vmem_limit_bytes=VMEM_BYTES),
        cost_estimate=pl.CostEstimate(
            flops=couplings * 16 * rows * rows * columns, bytes_accessed=4 * couplings * rows * columns, transcendentals=0),
        name="local_products",
    )(col_ref, coarse_tile, p_tiles, a_tiles)

    total = pl.pallas_call(
        halo_kernel,
        out_shape=jax.ShapeDtypeStruct((CT,) + tile, jnp.float32),
        in_specs=[smem_spec, any_spec, vmem_spec, vmem_spec, vmem_spec],
        out_specs=vmem_spec,
        scratch_shapes=[pltpu.SemaphoreType.DMA],
        compiler_params=pltpu.CompilerParams(vmem_limit_bytes=VMEM_BYTES),
        name="halo_products",
    )(place, partial, left, lower, upper)
    return group_sum(total)


def solution(mesh):
    in_specs = (
        P(("group", "bulk"), None, None),
        P(("group", "bulk"), None, None, None),
        P(("group", "bulk"), None),
        P(("group", "bulk"), None, None),
        P(("group", "bulk"), None),
    )
    out_specs = P("group", None, None)
    return jax.shard_map(shards, mesh=mesh, in_specs=in_specs, out_specs=out_specs, check_vma=False)
```

```python
import functools

import jax
import jax.numpy as jnp
from jax import lax
from jax.experimental import pallas as pl
from jax.experimental.pallas import tpu as pltpu
from jax.sharding import PartitionSpec as P

CT = 128
STEP_BLOCKS = 4
CHUNKS = 8
VMEM_BYTES = 56 * 1024 * 1024
SUM_VMEM_BYTES = 44 * 1024 * 1024


def shifted(block, axis, distance):
    devices = range(lax.axis_size(axis))
    route = [(i - distance, i) for i in devices if i - distance in devices]
    return lax.ppermute(block, axis, route)


def halves(x):
    high = x.astype(jnp.bfloat16)
    low = (x - high.astype(jnp.float32)).astype(jnp.bfloat16)
    return high, low


def left_form(x):
    return jnp.concatenate(halves(x), axis=1)


def right_form(x):
    row = jnp.concatenate(halves(x), axis=1)
    return jnp.concatenate([row, row], axis=0)


def product(left, right):
    both = jnp.dot(left, right, preferred_element_type=jnp.float32)
    width = both.shape[1] // 2
    return both[:, :width] + both[:, width:]


def pick_kernel(send_ref, p_ref, below_ref, above_ref):
    for side, target in enumerate((below_ref, above_ref)):
        @pl.loop(0, target.shape[0])
        def _(j):
            target[j] = p_ref[jnp.maximum(send_ref[0, side, j], 0)]


def local_kernel(col_ref, tile_ref, p_ref, a_ref, sum_ref, left_ref, before_ref, last_ref, right_p, place_ref):
    blocks = p_ref.shape[0]
    neighbours = a_ref.shape[1]
    slots = left_ref.shape[0] - 1
    step = pl.program_id(0)

    @pl.when(step == 0)
    def _():
        @pl.loop(0, blocks)
        def _(f):
            right_p[f] = right_form(p_ref[f])

        @pl.loop(0, sum_ref.shape[0])
        def _(t):
            sum_ref[t] = jnp.zeros(sum_ref.shape[1:], jnp.float32)

        @pl.loop(0, slots + 1)
        def _(j):
            place_ref[j] = -1

    for i in range(STEP_BLOCKS):
        f = step * STEP_BLOCKS + i
        p_left = left_form(p_ref[f].T)
        for k in range(neighbours):
            v = col_ref[k, f]
            t = tile_ref[k, f]
            local = v < blocks
            slot = jnp.where(local, slots, v - blocks)
            left = product(p_left, right_form(a_ref[i, k]))
            left_cat = left_form(left)
            left_ref[slot] = left_cat
            place_ref[slot] = t
            triple = product(left_cat, right_p[jnp.minimum(v, blocks - 1)])
            sum_ref[t] += jnp.where(local, triple, 0.0)

    @pl.when(step == pl.num_programs(0) - 1)
    def _():
        @pl.loop(0, last_ref.shape[0])
        def _(t):
            last_ref[t] = slots

        @pl.loop(0, slots)
        def _(j):
            t = place_ref[j]
            before_ref[j] = slots

            @pl.when(t >= 0)
            def _():
                before_ref[j] = last_ref[t]
                last_ref[t] = j


def reduce_kernel(orders, before_ref, last_ref, part_ref, left_ref, lower_ref, upper_ref, out_ref, mine, chain, *rest):
    stages = len(orders[0])
    bufs = rest[:stages]
    load_sem, send_sem, recv_sem = rest[stages:]
    me = lax.axis_index("bulk")
    tiles = part_ref.shape[0]
    chunks = CHUNKS
    capacity = lower_ref.shape[0]
    slots = 2 * capacity
    width = tiles // chunks
    ways = len(orders)
    bit = [(me // 2**b) % 2 for b in range(stages)]
    partner = [me + 2**b * (1 - 2 * bit[b]) for b in range(stages)]

    def load(c, way):
        here = pl.ds(c * width, width)
        return pltpu.make_async_copy(part_ref.at[here], mine.at[here], load_sem.at[c])

    def keep(c, way, s):
        at = c * width
        size = width
        for level in range(s + 1):
            size //= 2
            at = at + bit[orders[way][level]] * size
        return at, size

    def scatter(c, way, s):
        b = orders[way][s]
        size = width >> (s + 1)
        if s == 0:
            src = mine.at[pl.ds(c * width + (1 - bit[b]) * size, size)]
        else:
            src = bufs[s - 1].at[c, pl.ds((1 - bit[b]) * size, size)]
        return pltpu.make_async_remote_copy(
            src_ref=src, dst_ref=bufs[s].at[c], send_sem=send_sem.at[s, c], recv_sem=recv_sem.at[s, c],
            device_id={"bulk": partner[b]}, device_id_type=pl.DeviceIdType.MESH)

    def gather(c, way, s):
        b = orders[way][s]
        at, size = keep(c, way, s)
        region = out_ref.at[pl.ds(at, size)]
        n = 2 * stages - 1 - s
        return pltpu.make_async_remote_copy(
            src_ref=region, dst_ref=region, send_sem=send_sem.at[n, c], recv_sem=recv_sem.at[n, c],
            device_id={"bulk": partner[b]}, device_id_type=pl.DeviceIdType.MESH)

    def add(c, way, s):
        b = orders[way][s]
        size = width >> (s + 1)
        at, _ = keep(c, way, s)

        @pl.loop(0, size)
        def _(j):
            if s == 0:
                own = mine[c * width + bit[b] * size + j]
            else:
                own = bufs[s - 1][c, bit[b] * size + j]
            total = bufs[s][c, j] + own
            if s == stages - 1:
                out_ref[at + j] = total
            else:
                bufs[s][c, j] = total

    def each(body):
        @pl.loop(0, chunks // ways)
        def _(g):
            for way in range(ways):
                body(g * ways + way, way)

    each(lambda c, way: load(c, way).start())
    barrier = pltpu.get_barrier_semaphore()
    for b in range(stages):
        pl.semaphore_signal(barrier, inc=1, device_id={"bulk": partner[b]}, device_id_type=pl.DeviceIdType.MESH)

    chain[slots] = jnp.zeros(chain.shape[1:], jnp.float32)
    for side, tiles_ref in enumerate((lower_ref, upper_ref)):
        @pl.loop(0, capacity // 4)
        def _(group):
            for i in range(4):
                j = group * 4 + i
                slot = side * capacity + j
                triple = product(left_ref[slot], right_form(tiles_ref[j]))
                chain[slot] = triple + chain[before_ref[slot]]

    pl.semaphore_wait(barrier, stages)

    def finish(c, way):
        load(c, way).wait()

        @pl.loop(0, width)
        def _(i):
            t = c * width + i
            mine[t] += chain[last_ref[t]]
        scatter(c, way, 0).start()
    each(finish)
    for s in range(stages):
        def reduce_step(c, way, s=s):
            scatter(c, way, s).wait_recv()
            add(c, way, s)
            if s + 1 < stages:
                scatter(c, way, s + 1).start()
            else:
                gather(c, way, s).start()
        each(reduce_step)
    for s in reversed(range(stages)):
        def spread_step(c, way, s=s):
            gather(c, way, s).wait_recv()
            if s > 0:
                gather(c, way, s - 1).start()
        each(spread_step)

    def drain(c, way):
        for s in range(stages):
            scatter(c, way, s).wait_send()
            gather(c, way, s).wait_send()
    each(drain)


def group_sum(before, last, partial, left, lower, upper):
    devices = lax.axis_size("bulk")
    stages = devices.bit_length() - 1
    tiles, rows, columns = partial.shape
    width = tiles // CHUNKS
    bits = tuple(range(stages))
    if stages % 2:
        half = (stages - 1) // 2
        orders = (bits, bits[:1] + bits[1 + half:] + bits[1:1 + half])
    else:
        orders = (bits, bits[stages // 2:] + bits[:stages // 2])
    tile = (rows, columns)
    smem_spec = pl.BlockSpec(memory_space=pltpu.SMEM)
    vmem_spec = pl.BlockSpec(memory_space=pltpu.VMEM)
    vmem = functools.partial(pltpu.VMEM, dtype=jnp.float32)
    return pl.pallas_call(
        functools.partial(reduce_kernel, orders),
        out_shape=pltpu.VMEM(partial.shape, jnp.float32),
        in_specs=[smem_spec, smem_spec, pl.BlockSpec(memory_space=pl.ANY), vmem_spec, vmem_spec, vmem_spec],
        out_specs=vmem_spec,
        scratch_shapes=[vmem(partial.shape), vmem((2 * lower.shape[0] + 1,) + tile)]
        + [vmem((CHUNKS, width >> (s + 1)) + tile) for s in range(stages)]
        + [
            pltpu.SemaphoreType.DMA((CHUNKS,)),
            pltpu.SemaphoreType.DMA((2 * stages, CHUNKS)),
            pltpu.SemaphoreType.DMA((2 * stages, CHUNKS)),
        ],
        compiler_params=pltpu.CompilerParams(
            collective_id=0, has_side_effects=True, vmem_limit_bytes=SUM_VMEM_BYTES),
        cost_estimate=pl.CostEstimate(flops=tiles * rows * columns, bytes_accessed=8 * tiles * rows * columns, transcendentals=0),
        name="group_sum",
    )(before, last, partial, left, lower, upper)


def shards(p_tiles, a_tiles, col_ref, send_list, coarse_tile):
    blocks, rows, columns = p_tiles.shape
    neighbours = a_tiles.shape[1]
    capacity = send_list.shape[2]
    slots = 2 * capacity
    tile = (rows, columns)
    smem_spec = pl.BlockSpec(memory_space=pltpu.SMEM)
    vmem_spec = pl.BlockSpec(memory_space=pltpu.VMEM)

    sent = jax.ShapeDtypeStruct((capacity,) + tile, jnp.float32)
    to_below, to_above = pl.pallas_call(
        pick_kernel,
        out_shape=(sent, sent),
        in_specs=[smem_spec, vmem_spec],
        out_specs=(vmem_spec, vmem_spec),
        name="pick",
    )(send_list, p_tiles)
    lower = shifted(to_above, ("group", "bulk"), 1)
    upper = shifted(to_below, ("group", "bulk"), -1)

    couplings = blocks * neighbours
    whole = lambda *shape: pl.BlockSpec(shape, lambda s, *_: (0,) * len(shape))
    partial, left, before, last = pl.pallas_call(
        local_kernel,
        out_shape=(
            jax.ShapeDtypeStruct((CT,) + tile, jnp.float32),
            jax.ShapeDtypeStruct((slots + 1, rows, 2 * columns), jnp.bfloat16),
            jax.ShapeDtypeStruct((slots,), jnp.int32),
            jax.ShapeDtypeStruct((CT,), jnp.int32),
        ),
        grid_spec=pltpu.PrefetchScalarGridSpec(
            num_scalar_prefetch=2,
            grid=(blocks // STEP_BLOCKS,),
            in_specs=[
                whole(blocks, *tile),
                pl.BlockSpec((STEP_BLOCKS, neighbours) + tile, lambda s, *_: (s, 0, 0, 0)),
            ],
            out_specs=(whole(CT, *tile), whole(slots + 1, rows, 2 * columns), smem_spec, smem_spec),
            scratch_shapes=[pltpu.VMEM((blocks, 2 * rows, 2 * columns), jnp.bfloat16), pltpu.SMEM((slots + 1,), jnp.int32)],
        ),
        compiler_params=pltpu.CompilerParams(vmem_limit_bytes=VMEM_BYTES),
        cost_estimate=pl.CostEstimate(
            flops=couplings * 16 * rows * rows * columns, bytes_accessed=4 * couplings * rows * columns, transcendentals=0),
        name="local_products",
    )(col_ref.T, coarse_tile.T, p_tiles, a_tiles)

    return group_sum(before, last, partial, left, lower, upper)


def solution(mesh):
    in_specs = (
        P(("group", "bulk"), None, None),
        P(("group", "bulk"), None, None, None),
        P(("group", "bulk"), None),
        P(("group", "bulk"), None, None),
        P(("group", "bulk"), None),
    )
    out_specs = P("group", None, None)
    return jax.shard_map(shards, mesh=mesh, in_specs=in_specs, out_specs=out_specs, check_vma=False)
```

```python
import functools

import jax
import jax.numpy as jnp
from jax import lax
from jax.experimental import pallas as pl
from jax.experimental.pallas import tpu as pltpu
from jax.sharding import PartitionSpec as P

CT = 128
STEP_BLOCKS = 4
CHUNKS = 16
PIECE = 8
VMEM_BYTES = 52 * 1024 * 1024
SUM_VMEM_BYTES = 44 * 1024 * 1024


def shifted(block, axis, distance):
    devices = range(lax.axis_size(axis))
    route = [(i - distance, i) for i in devices if i - distance in devices]
    return lax.ppermute(block, axis, route)


def halves(x):
    high = x.astype(jnp.bfloat16)
    low = (x - high.astype(jnp.float32)).astype(jnp.bfloat16)
    return high, low


def left_form(x):
    return jnp.concatenate(halves(x), axis=1)


def right_form(x):
    row = jnp.concatenate(halves(x), axis=1)
    return jnp.concatenate([row, row], axis=0)


def product(left, right):
    both = jnp.dot(left, right, preferred_element_type=jnp.float32)
    width = both.shape[1] // 2
    return both[:, :width] + both[:, width:]


def pick_kernel(send_ref, p_ref, below_ref, above_ref, sem):
    def copy(side, target, j):
        row = jnp.maximum(send_ref[0, side, j], 0)
        return pltpu.make_async_copy(p_ref.at[row], target.at[j], sem.at[side, j])

    targets = ((1, above_ref), (0, below_ref))
    for side, target in targets:
        @pl.loop(0, target.shape[0])
        def _(j):
            copy(side, target, j).start()
    for side, target in targets:
        @pl.loop(0, target.shape[0])
        def _(j):
            copy(side, target, j).wait()


def local_kernel(col_ref, tile_ref, p_ref, a_ref, sum_ref, left_ref, link_ref, right_p, place_ref):
    blocks = p_ref.shape[0]
    neighbours = a_ref.shape[1]
    slots = left_ref.shape[0] - 1
    step = pl.program_id(0)

    @pl.when(step == 0)
    def _():
        @pl.loop(0, blocks)
        def _(f):
            right_p[f] = right_form(p_ref[f])

        @pl.loop(0, sum_ref.shape[0])
        def _(t):
            sum_ref[t] = jnp.zeros(sum_ref.shape[1:], jnp.float32)

        @pl.loop(0, slots + 1)
        def _(j):
            place_ref[j] = -1

    for i in range(STEP_BLOCKS):
        f = step * STEP_BLOCKS + i
        p_left = left_form(p_ref[f].T)
        for k in range(neighbours):
            v = col_ref[k, f]
            t = tile_ref[k, f]
            local = v < blocks
            slot = jnp.where(local, slots, v - blocks)
            left = product(p_left, right_form(a_ref[i, k]))
            left_cat = left_form(left)
            left_ref[slot] = left_cat
            place_ref[slot] = t
            triple = product(left_cat, right_p[jnp.minimum(v, blocks - 1)])
            sum_ref[t] += jnp.where(local, triple, 0.0)

    @pl.when(step == pl.num_programs(0) - 1)
    def _():
        @pl.loop(0, sum_ref.shape[0])
        def _(t):
            link_ref[slots + t] = slots

        @pl.loop(0, slots)
        def _(j):
            t = place_ref[j]
            link_ref[j] = slots

            @pl.when(t >= 0)
            def _():
                link_ref[j] = link_ref[slots + t]
                link_ref[slots + t] = j


def lower_kernel(link_ref, left_ref, lower_ref, chain_ref):
    group = lower_ref.shape[0]
    capacity = chain_ref.shape[0] - 1
    step = pl.program_id(0)

    @pl.when(step == 0)
    def _():
        chain_ref[capacity] = jnp.zeros(chain_ref.shape[1:], jnp.float32)

    for i in range(group):
        slot = step * group + i
        triple = product(left_ref[i], right_form(lower_ref[i]))
        chain_ref[slot] = triple + chain_ref[jnp.minimum(link_ref[slot], capacity)]


def reduce_kernel(orders, link_hbm, part_ref, left_hbm, lower_hbm, upper, out_ref, link_ref, left, mine, chain, *rest):
    stages = len(orders[0])
    bufs = rest[:stages]
    load_sem, halo_sem, send_sem, recv_sem = rest[stages:]
    me = lax.axis_index("bulk")
    tiles = part_ref.shape[0]
    chunks = load_sem.shape[0]
    capacity = upper.shape[0]
    pieces = capacity // PIECE
    slots = 2 * capacity
    width = tiles // chunks
    ways = len(orders)
    bit = [(me // 2**b) % 2 for b in range(stages)]
    partner = [me + 2**b * (1 - 2 * bit[b]) for b in range(stages)]

    def load(c, way):
        here = pl.ds(c * width, width)
        return pltpu.make_async_copy(part_ref.at[here], mine.at[here], load_sem.at[c])

    def keep(c, way, s):
        at = c * width
        size = width
        for level in range(s + 1):
            size //= 2
            at = at + bit[orders[way][level]] * size
        return at, size

    def scatter(c, way, s):
        b = orders[way][s]
        size = width >> (s + 1)
        if s == 0:
            src = mine.at[pl.ds(c * width + (1 - bit[b]) * size, size)]
        else:
            src = bufs[s - 1].at[c, pl.ds((1 - bit[b]) * size, size)]
        return pltpu.make_async_remote_copy(
            src_ref=src, dst_ref=bufs[s].at[c], send_sem=send_sem.at[s, c], recv_sem=recv_sem.at[s, c],
            device_id={"bulk": partner[b]}, device_id_type=pl.DeviceIdType.MESH)

    def gather(c, way, s):
        b = orders[way][s]
        at, size = keep(c, way, s)
        region = out_ref.at[pl.ds(at, size)]
        n = 2 * stages - 1 - s
        return pltpu.make_async_remote_copy(
            src_ref=region, dst_ref=region, send_sem=send_sem.at[n, c], recv_sem=recv_sem.at[n, c],
            device_id={"bulk": partner[b]}, device_id_type=pl.DeviceIdType.MESH)

    def add(c, way, s):
        b = orders[way][s]
        size = width >> (s + 1)
        at, _ = keep(c, way, s)

        @pl.loop(0, size)
        def _(j):
            if s == 0:
                own = mine[c * width + bit[b] * size + j]
            else:
                own = bufs[s - 1][c, bit[b] * size + j]
            total = bufs[s][c, j] + own
            if s == stages - 1:
                out_ref[at + j] = total
            else:
                bufs[s][c, j] = total

    def each(body):
        @pl.loop(0, chunks // ways)
        def _(g):
            for way in range(ways):
                body(g * ways + way, way)

    link_load = pltpu.make_async_copy(link_hbm, link_ref, halo_sem.at[pieces])
    lower_load = pltpu.make_async_copy(
        lower_hbm.at[pl.ds(0, capacity)], chain.at[pl.ds(0, capacity)], halo_sem.at[pieces + 1])

    def left_load(g):
        return pltpu.make_async_copy(
            left_hbm.at[pl.ds(capacity + g * PIECE, PIECE)], left.at[pl.ds(g * PIECE, PIECE)], halo_sem.at[g])

    link_load.start()
    for g in range(pieces):
        left_load(g).start()
    lower_load.start()
    each(lambda c, way: load(c, way).start())
    barrier = pltpu.get_barrier_semaphore()
    for b in range(stages):
        pl.semaphore_signal(barrier, inc=1, device_id={"bulk": partner[b]}, device_id_type=pl.DeviceIdType.MESH)

    chain[slots] = jnp.zeros(chain.shape[1:], jnp.float32)
    link_load.wait()
    lower_load.wait()

    @pl.loop(0, pieces)
    def _(g):
        left_load(g).wait()
        for i in range(PIECE):
            j = g * PIECE + i
            triple = product(left[j], right_form(upper[j]))
            chain[capacity + j] = triple + chain[link_ref[capacity + j]]

    pl.semaphore_wait(barrier, stages)

    def finish(c, way):
        load(c, way).wait()

        @pl.loop(0, width)
        def _(i):
            t = c * width + i
            mine[t] += chain[link_ref[slots + t]]
        scatter(c, way, 0).start()
    each(finish)
    for s in range(stages):
        def reduce_step(c, way, s=s):
            scatter(c, way, s).wait_recv()
            add(c, way, s)
            if s + 1 < stages:
                scatter(c, way, s + 1).start()
            else:
                gather(c, way, s).start()
        each(reduce_step)
    for s in reversed(range(stages)):
        def spread_step(c, way, s=s):
            gather(c, way, s).wait_recv()
            if s > 0:
                gather(c, way, s - 1).start()
        each(spread_step)

    def drain(c, way):
        for s in range(stages):
            scatter(c, way, s).wait_send()
            gather(c, way, s).wait_send()
    each(drain)


def group_sum(links, partial, left, lower, upper):
    devices = lax.axis_size("bulk")
    stages = devices.bit_length() - 1
    tiles, rows, columns = partial.shape
    chunks = min(CHUNKS, tiles // devices)
    width = tiles // chunks
    capacity = upper.shape[0]
    bits = tuple(range(stages))
    if stages % 2:
        half = (stages - 1) // 2
        orders = (bits, bits[:1] + bits[1 + half:] + bits[1:1 + half])
    else:
        orders = (bits, bits[stages // 2:] + bits[:stages // 2])
    tile = (rows, columns)
    hbm_spec = pl.BlockSpec(memory_space=pltpu.HBM)
    vmem = functools.partial(pltpu.VMEM, dtype=jnp.float32)
    return pl.pallas_call(
        functools.partial(reduce_kernel, orders),
        out_shape=pltpu.VMEM(partial.shape, jnp.float32),
        in_specs=[hbm_spec] * 4 + [pl.BlockSpec(memory_space=pltpu.VMEM)],
        out_specs=pl.BlockSpec(memory_space=pltpu.VMEM),
        scratch_shapes=[
            pltpu.SMEM(links.shape, jnp.int32),
            pltpu.VMEM((capacity,) + left.shape[1:], left.dtype),
            vmem(partial.shape),
            vmem((2 * capacity + 1,) + tile),
        ]
        + [vmem((chunks, width >> (s + 1)) + tile) for s in range(stages)]
        + [
            pltpu.SemaphoreType.DMA((chunks,)),
            pltpu.SemaphoreType.DMA((capacity // PIECE + 2,)),
            pltpu.SemaphoreType.DMA((2 * stages, chunks)),
            pltpu.SemaphoreType.DMA((2 * stages, chunks)),
        ],
        compiler_params=pltpu.CompilerParams(
            collective_id=0, has_side_effects=True, vmem_limit_bytes=SUM_VMEM_BYTES),
        cost_estimate=pl.CostEstimate(flops=tiles * rows * columns, bytes_accessed=8 * tiles * rows * columns, transcendentals=0),
        name="group_sum",
    )(links, partial, left, lower, upper)


def shards(p_tiles, a_tiles, col_ref, send_list, coarse_tile):
    blocks, rows, columns = p_tiles.shape
    neighbours = a_tiles.shape[1]
    capacity = send_list.shape[2]
    slots = 2 * capacity
    tile = (rows, columns)
    smem_spec = pl.BlockSpec(memory_space=pltpu.SMEM)
    vmem_spec = pl.BlockSpec(memory_space=pltpu.VMEM)
    hbm_spec = pl.BlockSpec(memory_space=pltpu.HBM)

    sent = pltpu.VMEM((capacity,) + tile, jnp.float32)
    to_below, to_above = pl.pallas_call(
        pick_kernel,
        out_shape=(sent, sent),
        in_specs=[smem_spec, hbm_spec],
        out_specs=(vmem_spec, vmem_spec),
        scratch_shapes=[pltpu.SemaphoreType.DMA((2, capacity))],
        compiler_params=pltpu.CompilerParams(vmem_limit_bytes=8 * 1024 * 1024),
        name="pick",
    )(send_list, pltpu.with_memory_space_constraint(p_tiles, pltpu.HBM))
    lower = shifted(to_above, ("group", "bulk"), 1)
    upper = shifted(to_below, ("group", "bulk"), -1)

    couplings = blocks * neighbours
    whole = lambda *shape: pl.BlockSpec(shape, lambda s, *_: (0,) * len(shape))
    partial, left, links = pl.pallas_call(
        local_kernel,
        out_shape=(
            jax.ShapeDtypeStruct((CT,) + tile, jnp.float32),
            jax.ShapeDtypeStruct((slots + 1, rows, 2 * columns), jnp.bfloat16),
            jax.ShapeDtypeStruct((-(-(slots + CT) // 128) * 128,), jnp.int32),
        ),
        grid_spec=pltpu.PrefetchScalarGridSpec(
            num_scalar_prefetch=2,
            grid=(blocks // STEP_BLOCKS,),
            in_specs=[
                whole(blocks, *tile),
                pl.BlockSpec((STEP_BLOCKS, neighbours) + tile, lambda s, *_: (s, 0, 0, 0)),
            ],
            out_specs=(whole(CT, *tile), whole(slots + 1, rows, 2 * columns), smem_spec),
            scratch_shapes=[pltpu.VMEM((blocks, 2 * rows, 2 * columns), jnp.bfloat16), pltpu.SMEM((slots + 1,), jnp.int32)],
        ),
        compiler_params=pltpu.CompilerParams(vmem_limit_bytes=VMEM_BYTES),
        cost_estimate=pl.CostEstimate(
            flops=couplings * 16 * rows * rows * columns, bytes_accessed=4 * couplings * rows * columns, transcendentals=0),
        name="local_products",
    )(col_ref.T, coarse_tile.T, p_tiles, a_tiles)

    lower_chain = pl.pallas_call(
        lower_kernel,
        out_shape=pltpu.HBM((capacity + 1,) + tile, jnp.float32),
        grid_spec=pltpu.PrefetchScalarGridSpec(
            num_scalar_prefetch=1,
            grid=(capacity // PIECE,),
            in_specs=[
                pl.BlockSpec((PIECE, rows, 2 * columns), lambda s, *_: (s, 0, 0)),
                pl.BlockSpec((PIECE,) + tile, lambda s, *_: (s, 0, 0)),
            ],
            out_specs=whole(capacity + 1, *tile),
        ),
        compiler_params=pltpu.CompilerParams(vmem_limit_bytes=24 * 1024 * 1024),
        cost_estimate=pl.CostEstimate(
            flops=capacity * 8 * rows * rows * columns, bytes_accessed=12 * capacity * rows * columns, transcendentals=0),
        name="lower_products",
    )(links, left, lower)
    return group_sum(links, partial, left, lower_chain, pltpu.with_memory_space_constraint(upper, pltpu.VMEM))


def solution(mesh):
    in_specs = (
        P(("group", "bulk"), None, None),
        P(("group", "bulk"), None, None, None),
        P(("group", "bulk"), None),
        P(("group", "bulk"), None, None),
        P(("group", "bulk"), None),
    )
    out_specs = P("group", None, None)
    return jax.shard_map(shards, mesh=mesh, in_specs=in_specs, out_specs=out_specs, check_vma=False)
```

```python
import functools

import jax
import jax.numpy as jnp
from jax import lax
from jax.experimental import pallas as pl
from jax.experimental.pallas import tpu as pltpu
from jax.sharding import PartitionSpec as P

CT = 128
STEP_BLOCKS = 4
CHUNKS = 16
PIECE = 8
VMEM_BYTES = 52 * 1024 * 1024
SUM_VMEM_BYTES = 44 * 1024 * 1024


def shifted(block, axis, distance):
    devices = range(lax.axis_size(axis))
    route = [(i - distance, i) for i in devices if i - distance in devices]
    return lax.ppermute(block, axis, route)


def halves(x):
    high = x.astype(jnp.bfloat16)
    low = (x - high.astype(jnp.float32)).astype(jnp.bfloat16)
    return high, low


def left_form(x):
    return jnp.concatenate(halves(x), axis=1)


def right_form(x):
    row = jnp.concatenate(halves(x), axis=1)
    return jnp.concatenate([row, row], axis=0)


def product(left, right):
    both = jnp.dot(left, right, preferred_element_type=jnp.float32)
    width = both.shape[1] // 2
    return both[:, :width] + both[:, width:]


def pick_kernel(side, send_ref, p_ref, out_ref, sem):
    def copy(j):
        row = jnp.maximum(send_ref[0, side, j], 0)
        return pltpu.make_async_copy(p_ref.at[row], out_ref.at[j], sem.at[j])

    @pl.loop(0, out_ref.shape[0] // 4)
    def _(g):
        for i in range(4):
            copy(g * 4 + i).start()

    @pl.loop(0, out_ref.shape[0])
    def _(j):
        copy(j).wait()


def local_kernel(col_ref, tile_ref, p_ref, a_ref, sum_ref, left_ref, link_ref, right_p, place_ref):
    blocks = p_ref.shape[0]
    neighbours = a_ref.shape[1]
    slots = left_ref.shape[0] - 1
    step = pl.program_id(0)

    @pl.when(step == 0)
    def _():
        @pl.loop(0, blocks)
        def _(f):
            right_p[f] = right_form(p_ref[f])

        @pl.loop(0, sum_ref.shape[0])
        def _(t):
            sum_ref[t] = jnp.zeros(sum_ref.shape[1:], jnp.float32)

        @pl.loop(0, slots + 1)
        def _(j):
            place_ref[j] = -1

    for i in range(STEP_BLOCKS):
        f = step * STEP_BLOCKS + i
        p_left = left_form(p_ref[f].T)
        for k in range(neighbours):
            v = col_ref[k, f]
            t = tile_ref[k, f]
            local = v < blocks
            slot = jnp.where(local, slots, v - blocks)
            left = product(p_left, right_form(a_ref[i, k]))
            left_cat = left_form(left)
            left_ref[slot] = left_cat
            place_ref[slot] = t
            triple = product(left_cat, right_p[jnp.minimum(v, blocks - 1)])
            sum_ref[t] += jnp.where(local, triple, 0.0)

    @pl.when(step == pl.num_programs(0) - 1)
    def _():
        @pl.loop(0, sum_ref.shape[0])
        def _(t):
            link_ref[slots + t] = slots

        @pl.loop(0, slots)
        def _(j):
            t = place_ref[j]
            link_ref[j] = slots

            @pl.when(t >= 0)
            def _():
                link_ref[j] = link_ref[slots + t]
                link_ref[slots + t] = j


def reduce_kernel(orders, link_hbm, part_ref, left_hbm, lower, upper, out_ref, link_ref, left, mine, chain, *rest):
    stages = len(orders[0])
    bufs = rest[:stages]
    load_sem, halo_sem, send_sem, recv_sem = rest[stages:]
    me = lax.axis_index("bulk")
    tiles = part_ref.shape[0]
    chunks = load_sem.shape[0]
    capacity = upper.shape[0]
    slots = 2 * capacity
    pieces = slots // PIECE
    width = tiles // chunks
    ways = len(orders)
    bit = [(me // 2**b) % 2 for b in range(stages)]
    partner = [me + 2**b * (1 - 2 * bit[b]) for b in range(stages)]

    def load(c, way):
        here = pl.ds(c * width, width)
        return pltpu.make_async_copy(part_ref.at[here], mine.at[here], load_sem.at[c])

    def keep(c, way, s):
        at = c * width
        size = width
        for level in range(s + 1):
            size //= 2
            at = at + bit[orders[way][level]] * size
        return at, size

    def scatter(c, way, s):
        b = orders[way][s]
        size = width >> (s + 1)
        if s == 0:
            src = mine.at[pl.ds(c * width + (1 - bit[b]) * size, size)]
        else:
            src = bufs[s - 1].at[c, pl.ds((1 - bit[b]) * size, size)]
        return pltpu.make_async_remote_copy(
            src_ref=src, dst_ref=bufs[s].at[c], send_sem=send_sem.at[s, c], recv_sem=recv_sem.at[s, c],
            device_id={"bulk": partner[b]}, device_id_type=pl.DeviceIdType.MESH)

    def gather(c, way, s):
        b = orders[way][s]
        at, size = keep(c, way, s)
        region = out_ref.at[pl.ds(at, size)]
        n = 2 * stages - 1 - s
        return pltpu.make_async_remote_copy(
            src_ref=region, dst_ref=region, send_sem=send_sem.at[n, c], recv_sem=recv_sem.at[n, c],
            device_id={"bulk": partner[b]}, device_id_type=pl.DeviceIdType.MESH)

    def add(c, way, s):
        b = orders[way][s]
        size = width >> (s + 1)
        at, _ = keep(c, way, s)

        @pl.loop(0, size)
        def _(j):
            if s == 0:
                own = mine[c * width + bit[b] * size + j]
            else:
                own = bufs[s - 1][c, bit[b] * size + j]
            total = bufs[s][c, j] + own
            if s == stages - 1:
                out_ref[at + j] = total
            else:
                bufs[s][c, j] = total

    def each(body):
        @pl.loop(0, chunks // ways)
        def _(g):
            for way in range(ways):
                body(g * ways + way, way)

    link_load = pltpu.make_async_copy(link_hbm, link_ref, halo_sem.at[pieces])

    def left_load(g):
        return pltpu.make_async_copy(
            left_hbm.at[pl.ds(g * PIECE, PIECE)], left.at[pl.ds(g * PIECE, PIECE)], halo_sem.at[g])

    link_load.start()
    for g in range(pieces):
        left_load(g).start()
    each(lambda c, way: load(c, way).start())
    barrier = pltpu.get_barrier_semaphore()
    for b in range(stages):
        pl.semaphore_signal(barrier, inc=1, device_id={"bulk": partner[b]}, device_id_type=pl.DeviceIdType.MESH)

    chain[slots] = jnp.zeros(chain.shape[1:], jnp.float32)
    link_load.wait()

    for side, arrived in enumerate((lower, upper)):
        @pl.loop(0, capacity // PIECE)
        def _(g, side=side, arrived=arrived):
            left_load(side * (capacity // PIECE) + g).wait()
            for i in range(PIECE):
                j = g * PIECE + i
                slot = side * capacity + j
                triple = product(left[slot], right_form(arrived[j]))
                chain[slot] = triple + chain[link_ref[slot]]

    pl.semaphore_wait(barrier, stages)

    def finish(c, way):
        load(c, way).wait()

        @pl.loop(0, width)
        def _(i):
            t = c * width + i
            mine[t] += chain[link_ref[slots + t]]
        scatter(c, way, 0).start()
    each(finish)
    for s in range(stages):
        def reduce_step(c, way, s=s):
            scatter(c, way, s).wait_recv()
            add(c, way, s)
            if s + 1 < stages:
                scatter(c, way, s + 1).start()
            else:
                gather(c, way, s).start()
        each(reduce_step)
    for s in reversed(range(stages)):
        def spread_step(c, way, s=s):
            gather(c, way, s).wait_recv()
            if s > 0:
                gather(c, way, s - 1).start()
        each(spread_step)

    def drain(c, way):
        for s in range(stages):
            scatter(c, way, s).wait_send()
            gather(c, way, s).wait_send()
    each(drain)


def group_sum(links, partial, left, lower, upper):
    devices = lax.axis_size("bulk")
    stages = devices.bit_length() - 1
    tiles, rows, columns = partial.shape
    chunks = min(CHUNKS, tiles // devices)
    width = tiles // chunks
    capacity = upper.shape[0]
    bits = tuple(range(stages))
    if stages % 2:
        half = (stages - 1) // 2
        orders = (bits, bits[:1] + bits[1 + half:] + bits[1:1 + half])
    else:
        orders = (bits, bits[stages // 2:] + bits[:stages // 2])
    tile = (rows, columns)
    hbm_spec = pl.BlockSpec(memory_space=pltpu.HBM)
    vmem_spec = pl.BlockSpec(memory_space=pltpu.VMEM)
    vmem = functools.partial(pltpu.VMEM, dtype=jnp.float32)
    return pl.pallas_call(
        functools.partial(reduce_kernel, orders),
        out_shape=pltpu.VMEM(partial.shape, jnp.float32),
        in_specs=[hbm_spec] * 3 + [vmem_spec] * 2,
        out_specs=vmem_spec,
        scratch_shapes=[
            pltpu.SMEM(links.shape, jnp.int32),
            pltpu.VMEM((2 * capacity,) + left.shape[1:], left.dtype),
            vmem(partial.shape),
            vmem((2 * capacity + 1,) + tile),
        ]
        + [vmem((chunks, width >> (s + 1)) + tile) for s in range(stages)]
        + [
            pltpu.SemaphoreType.DMA((chunks,)),
            pltpu.SemaphoreType.DMA((2 * capacity // PIECE + 1,)),
            pltpu.SemaphoreType.DMA((2 * stages, chunks)),
            pltpu.SemaphoreType.DMA((2 * stages, chunks)),
        ],
        compiler_params=pltpu.CompilerParams(
            collective_id=0, has_side_effects=True, vmem_limit_bytes=SUM_VMEM_BYTES),
        cost_estimate=pl.CostEstimate(flops=tiles * rows * columns, bytes_accessed=8 * tiles * rows * columns, transcendentals=0),
        name="group_sum",
    )(links, partial, left, lower, upper)


def shards(p_tiles, a_tiles, col_ref, send_list, coarse_tile):
    blocks, rows, columns = p_tiles.shape
    neighbours = a_tiles.shape[1]
    capacity = send_list.shape[2]
    slots = 2 * capacity
    tile = (rows, columns)
    smem_spec = pl.BlockSpec(memory_space=pltpu.SMEM)
    vmem_spec = pl.BlockSpec(memory_space=pltpu.VMEM)
    hbm_spec = pl.BlockSpec(memory_space=pltpu.HBM)

    def picked(side, name):
        return pl.pallas_call(
            functools.partial(pick_kernel, side),
            out_shape=pltpu.VMEM((capacity,) + tile, jnp.float32),
            in_specs=[smem_spec, hbm_spec],
            out_specs=vmem_spec,
            scratch_shapes=[pltpu.SemaphoreType.DMA((capacity,))],
            compiler_params=pltpu.CompilerParams(vmem_limit_bytes=8 * 1024 * 1024),
            name=name,
        )(send_list, pltpu.with_memory_space_constraint(p_tiles, pltpu.HBM))

    lower = shifted(picked(1, "pick_above"), ("group", "bulk"), 1)
    upper = shifted(picked(0, "pick_below"), ("group", "bulk"), -1)

    couplings = blocks * neighbours
    whole = lambda *shape: pl.BlockSpec(shape, lambda s, *_: (0,) * len(shape))
    partial, left, links = pl.pallas_call(
        local_kernel,
        out_shape=(
            jax.ShapeDtypeStruct((CT,) + tile, jnp.float32),
            jax.ShapeDtypeStruct((slots + 1, rows, 2 * columns), jnp.bfloat16),
            jax.ShapeDtypeStruct((-(-(slots + CT) // 128) * 128,), jnp.int32),
        ),
        grid_spec=pltpu.PrefetchScalarGridSpec(
            num_scalar_prefetch=2,
            grid=(blocks // STEP_BLOCKS,),
            in_specs=[
                whole(blocks, *tile),
                pl.BlockSpec((STEP_BLOCKS, neighbours) + tile, lambda s, *_: (s, 0, 0, 0)),
            ],
            out_specs=(whole(CT, *tile), whole(slots + 1, rows, 2 * columns), smem_spec),
            scratch_shapes=[pltpu.VMEM((blocks, 2 * rows, 2 * columns), jnp.bfloat16), pltpu.SMEM((slots + 1,), jnp.int32)],
        ),
        compiler_params=pltpu.CompilerParams(vmem_limit_bytes=VMEM_BYTES),
        cost_estimate=pl.CostEstimate(
            flops=couplings * 16 * rows * rows * columns, bytes_accessed=4 * couplings * rows * columns, transcendentals=0),
        name="local_products",
    )(col_ref.T, coarse_tile.T, p_tiles, a_tiles)

    lower, upper = (pltpu.with_memory_space_constraint(x, pltpu.VMEM) for x in (lower, upper))
    return group_sum(links, partial, left, lower, upper)


def solution(mesh):
    in_specs = (
        P(("group", "bulk"), None, None),
        P(("group", "bulk"), None, None, None),
        P(("group", "bulk"), None),
        P(("group", "bulk"), None, None),
        P(("group", "bulk"), None),
    )
    out_specs = P("group", None, None)
    return jax.shard_map(shards, mesh=mesh, in_specs=in_specs, out_specs=out_specs, check_vma=False)
```

```python
import functools

import jax
import jax.numpy as jnp
from jax import lax
from jax.experimental import pallas as pl
from jax.experimental.pallas import tpu as pltpu
from jax.sharding import PartitionSpec as P

CT = 128
STEP_BLOCKS = 4
CHUNKS = 16
PIECE = 8
VMEM_BYTES = 52 * 1024 * 1024
SUM_VMEM_BYTES = 44 * 1024 * 1024


def shifted(block, axis, distance):
    devices = range(lax.axis_size(axis))
    route = [(i - distance, i) for i in devices if i - distance in devices]
    return lax.ppermute(block, axis, route)


def halves(x):
    high = x.astype(jnp.bfloat16)
    low = (x - high.astype(jnp.float32)).astype(jnp.bfloat16)
    return high, low


def left_form(x):
    return jnp.concatenate(halves(x), axis=1)


def right_form(x):
    row = jnp.concatenate(halves(x), axis=1)
    return jnp.concatenate([row, row], axis=0)


def product(left, right):
    both = jnp.dot(left, right, preferred_element_type=jnp.float32)
    width = both.shape[1] // 2
    return both[:, :width] + both[:, width:]


def pick_kernel(side, send_ref, p_ref, out_ref, sem):
    def copy(j):
        row = jnp.maximum(send_ref[0, side, j], 0)
        return pltpu.make_async_copy(p_ref.at[row], out_ref.at[j], sem.at[j])

    @pl.loop(0, out_ref.shape[0] // 4)
    def _(g):
        for i in range(4):
            copy(g * 4 + i).start()

    @pl.loop(0, out_ref.shape[0])
    def _(j):
        copy(j).wait()


def local_kernel(col_ref, tile_ref, p_ref, a_ref, sum_ref, left_ref, link_ref, right_p, place_ref):
    blocks = p_ref.shape[0]
    neighbours = a_ref.shape[1]
    slots = left_ref.shape[0] - 1
    step = pl.program_id(0)

    @pl.when(step == 0)
    def _():
        @pl.loop(0, blocks)
        def _(f):
            right_p[f] = right_form(p_ref[f])

        @pl.loop(0, sum_ref.shape[0])
        def _(t):
            sum_ref[t] = jnp.zeros(sum_ref.shape[1:], jnp.float32)

        @pl.loop(0, slots + 1)
        def _(j):
            place_ref[j] = -1

    for i in range(STEP_BLOCKS):
        f = step * STEP_BLOCKS + i
        p_left = left_form(p_ref[f].T)
        for k in range(neighbours):
            v = col_ref[k, f]
            t = tile_ref[k, f]
            local = v < blocks
            slot = jnp.where(local, slots, v - blocks)
            left = product(p_left, right_form(a_ref[i, k]))
            left_cat = left_form(left)
            left_ref[slot] = left_cat
            place_ref[slot] = t
            triple = product(left_cat, right_p[jnp.minimum(v, blocks - 1)])
            sum_ref[t] += jnp.where(local, triple, 0.0)

    @pl.when(step == pl.num_programs(0) - 1)
    def _():
        @pl.loop(0, sum_ref.shape[0])
        def _(t):
            link_ref[slots + t] = slots

        @pl.loop(0, slots)
        def _(j):
            t = place_ref[j]
            link_ref[j] = slots

            @pl.when(t >= 0)
            def _():
                link_ref[j] = link_ref[slots + t]
                link_ref[slots + t] = j


def reduce_kernel(orders, link_hbm, part_ref, left_hbm, lower, upper, out_ref, link_ref, left, mine, chain, *rest):
    stages = len(orders[0])
    bufs = rest[:stages]
    load_sem, halo_sem, send_sem, recv_sem = rest[stages:]
    me = lax.axis_index("bulk")
    tiles = part_ref.shape[0]
    chunks = load_sem.shape[0]
    capacity = upper.shape[0]
    slots = 2 * capacity
    pieces = slots // PIECE
    width = tiles // chunks
    ways = len(orders)
    bit = [(me // 2**b) % 2 for b in range(stages)]
    partner = [me + 2**b * (1 - 2 * bit[b]) for b in range(stages)]

    def load(c, way):
        here = pl.ds(c * width, width)
        return pltpu.make_async_copy(part_ref.at[here], mine.at[here], load_sem.at[c])

    def keep(c, way, s):
        at = c * width
        size = width
        for level in range(s + 1):
            size //= 2
            at = at + bit[orders[way][level]] * size
        return at, size

    def scatter(c, way, s):
        b = orders[way][s]
        size = width >> (s + 1)
        if s == 0:
            src = mine.at[pl.ds(c * width + (1 - bit[b]) * size, size)]
        else:
            src = bufs[s - 1].at[c, pl.ds((1 - bit[b]) * size, size)]
        return pltpu.make_async_remote_copy(
            src_ref=src, dst_ref=bufs[s].at[c], send_sem=send_sem.at[s, c], recv_sem=recv_sem.at[s, c],
            device_id={"bulk": partner[b]}, device_id_type=pl.DeviceIdType.MESH)

    def gather(c, way, s):
        b = orders[way][s]
        at, size = keep(c, way, s)
        region = out_ref.at[pl.ds(at, size)]
        n = 2 * stages - 1 - s
        return pltpu.make_async_remote_copy(
            src_ref=region, dst_ref=region, send_sem=send_sem.at[n, c], recv_sem=recv_sem.at[n, c],
            device_id={"bulk": partner[b]}, device_id_type=pl.DeviceIdType.MESH)

    def add(c, way, s):
        b = orders[way][s]
        size = width >> (s + 1)
        at, _ = keep(c, way, s)

        def add_tile(j):
            if s == 0:
                own = mine[c * width + bit[b] * size + j]
            else:
                own = bufs[s - 1][c, bit[b] * size + j]
            total = bufs[s][c, j] + own
            if s == stages - 1:
                out_ref[at + j] = total
            else:
                bufs[s][c, j] = total

        if size % 2:
            pl.loop(0, size)(add_tile)
        else:
            @pl.loop(0, size // 2)
            def _(g):
                add_tile(2 * g)
                add_tile(2 * g + 1)

    def each(body):
        @pl.loop(0, chunks // ways)
        def _(g):
            for way in range(ways):
                body(g * ways + way, way)

    link_load = pltpu.make_async_copy(link_hbm, link_ref, halo_sem.at[pieces])

    def left_load(g):
        return pltpu.make_async_copy(
            left_hbm.at[pl.ds(g * PIECE, PIECE)], left.at[pl.ds(g * PIECE, PIECE)], halo_sem.at[g])

    link_load.start()
    for g in range(pieces):
        left_load(g).start()
    each(lambda c, way: load(c, way).start())
    barrier = pltpu.get_barrier_semaphore()
    for b in range(stages):
        pl.semaphore_signal(barrier, inc=1, device_id={"bulk": partner[b]}, device_id_type=pl.DeviceIdType.MESH)

    chain[slots] = jnp.zeros(chain.shape[1:], jnp.float32)
    link_load.wait()

    for side, arrived in enumerate((lower, upper)):
        @pl.loop(0, capacity // PIECE)
        def _(g, side=side, arrived=arrived):
            left_load(side * (capacity // PIECE) + g).wait()
            for i in range(PIECE):
                j = g * PIECE + i
                slot = side * capacity + j
                triple = product(left[slot], right_form(arrived[j]))
                chain[slot] = triple + chain[link_ref[slot]]

    pl.semaphore_wait(barrier, stages)

    def finish(c, way):
        load(c, way).wait()

        @pl.loop(0, width // 4)
        def _(g):
            for i in range(4):
                t = c * width + g * 4 + i
                mine[t] += chain[link_ref[slots + t]]
        scatter(c, way, 0).start()

    def reduce_step(c, way, s):
        scatter(c, way, s).wait_recv()
        add(c, way, s)
        if s + 1 < stages:
            scatter(c, way, s + 1).start()
        else:
            gather(c, way, s).start()

    for way in range(ways):
        finish(way, way)

    @pl.loop(1, chunks // ways)
    def _(g):
        for way in range(ways):
            finish(g * ways + way, way)
        for way in range(ways):
            reduce_step((g - 1) * ways + way, way, 0)

    for way in range(ways):
        reduce_step(chunks - ways + way, way, 0)
    for s in range(1, stages):
        each(functools.partial(reduce_step, s=s))
    for s in reversed(range(stages)):
        def spread_step(c, way, s=s):
            gather(c, way, s).wait_recv()
            if s > 0:
                gather(c, way, s - 1).start()
        each(spread_step)

    def drain(c, way):
        for s in range(stages):
            scatter(c, way, s).wait_send()
            gather(c, way, s).wait_send()
    each(drain)


def group_sum(links, partial, left, lower, upper):
    devices = lax.axis_size("bulk")
    stages = devices.bit_length() - 1
    tiles, rows, columns = partial.shape
    chunks = min(CHUNKS, tiles // devices)
    width = tiles // chunks
    capacity = upper.shape[0]
    bits = tuple(range(stages))
    if stages % 2:
        half = (stages - 1) // 2
        orders = (bits, bits[:1] + bits[1 + half:] + bits[1:1 + half])
    else:
        orders = (bits, bits[stages // 2:] + bits[:stages // 2])
    tile = (rows, columns)
    hbm_spec = pl.BlockSpec(memory_space=pltpu.HBM)
    vmem_spec = pl.BlockSpec(memory_space=pltpu.VMEM)
    vmem = functools.partial(pltpu.VMEM, dtype=jnp.float32)
    return pl.pallas_call(
        functools.partial(reduce_kernel, orders),
        out_shape=pltpu.VMEM(partial.shape, jnp.float32),
        in_specs=[hbm_spec] * 3 + [vmem_spec] * 2,
        out_specs=vmem_spec,
        scratch_shapes=[
            pltpu.SMEM(links.shape, jnp.int32),
            pltpu.VMEM((2 * capacity,) + left.shape[1:], left.dtype),
            vmem(partial.shape),
            vmem((2 * capacity + 1,) + tile),
        ]
        + [vmem((chunks, width >> (s + 1)) + tile) for s in range(stages)]
        + [
            pltpu.SemaphoreType.DMA((chunks,)),
            pltpu.SemaphoreType.DMA((2 * capacity // PIECE + 1,)),
            pltpu.SemaphoreType.DMA((2 * stages, chunks)),
            pltpu.SemaphoreType.DMA((2 * stages, chunks)),
        ],
        compiler_params=pltpu.CompilerParams(
            collective_id=0, has_side_effects=True, vmem_limit_bytes=SUM_VMEM_BYTES),
        cost_estimate=pl.CostEstimate(flops=tiles * rows * columns, bytes_accessed=8 * tiles * rows * columns, transcendentals=0),
        name="group_sum",
    )(links, partial, left, lower, upper)


def shards(p_tiles, a_tiles, col_ref, send_list, coarse_tile):
    blocks, rows, columns = p_tiles.shape
    neighbours = a_tiles.shape[1]
    capacity = send_list.shape[2]
    slots = 2 * capacity
    tile = (rows, columns)
    smem_spec = pl.BlockSpec(memory_space=pltpu.SMEM)
    vmem_spec = pl.BlockSpec(memory_space=pltpu.VMEM)
    hbm_spec = pl.BlockSpec(memory_space=pltpu.HBM)

    def picked(side, name):
        return pl.pallas_call(
            functools.partial(pick_kernel, side),
            out_shape=pltpu.VMEM((capacity,) + tile, jnp.float32),
            in_specs=[smem_spec, hbm_spec],
            out_specs=vmem_spec,
            scratch_shapes=[pltpu.SemaphoreType.DMA((capacity,))],
            compiler_params=pltpu.CompilerParams(vmem_limit_bytes=8 * 1024 * 1024),
            name=name,
        )(send_list, pltpu.with_memory_space_constraint(p_tiles, pltpu.HBM))

    lower = shifted(picked(1, "pick_above"), ("group", "bulk"), 1)
    upper = shifted(picked(0, "pick_below"), ("group", "bulk"), -1)

    couplings = blocks * neighbours
    whole = lambda *shape: pl.BlockSpec(shape, lambda s, *_: (0,) * len(shape))
    partial, left, links = pl.pallas_call(
        local_kernel,
        out_shape=(
            jax.ShapeDtypeStruct((CT,) + tile, jnp.float32),
            jax.ShapeDtypeStruct((slots + 1, rows, 2 * columns), jnp.bfloat16),
            jax.ShapeDtypeStruct((-(-(slots + CT) // 128) * 128,), jnp.int32),
        ),
        grid_spec=pltpu.PrefetchScalarGridSpec(
            num_scalar_prefetch=2,
            grid=(blocks // STEP_BLOCKS,),
            in_specs=[
                whole(blocks, *tile),
                pl.BlockSpec((STEP_BLOCKS, neighbours) + tile, lambda s, *_: (s, 0, 0, 0)),
            ],
            out_specs=(whole(CT, *tile), whole(slots + 1, rows, 2 * columns), smem_spec),
            scratch_shapes=[pltpu.VMEM((blocks, 2 * rows, 2 * columns), jnp.bfloat16), pltpu.SMEM((slots + 1,), jnp.int32)],
        ),
        compiler_params=pltpu.CompilerParams(vmem_limit_bytes=VMEM_BYTES),
        cost_estimate=pl.CostEstimate(
            flops=couplings * 16 * rows * rows * columns, bytes_accessed=4 * couplings * rows * columns, transcendentals=0),
        name="local_products",
    )(col_ref.T, coarse_tile.T, p_tiles, a_tiles)

    lower, upper = (pltpu.with_memory_space_constraint(x, pltpu.VMEM) for x in (lower, upper))
    return group_sum(links, partial, left, lower, upper)


def solution(mesh):
    in_specs = (
        P(("group", "bulk"), None, None),
        P(("group", "bulk"), None, None, None),
        P(("group", "bulk"), None),
        P(("group", "bulk"), None, None),
        P(("group", "bulk"), None),
    )
    out_specs = P("group", None, None)
    return jax.shard_map(shards, mesh=mesh, in_specs=in_specs, out_specs=out_specs, check_vma=False)
```

```python
import functools

import jax
import jax.numpy as jnp
from jax import lax
from jax.experimental import pallas as pl
from jax.experimental.pallas import tpu as pltpu
from jax.sharding import PartitionSpec as P

CT = 128
STEP_BLOCKS = 4
CHUNKS = 16
PIECE = 8
VMEM_BYTES = 52 * 1024 * 1024
SUM_VMEM_BYTES = 44 * 1024 * 1024


def shifted(block, axis, distance):
    devices = range(lax.axis_size(axis))
    route = [(i - distance, i) for i in devices if i - distance in devices]
    return lax.ppermute(block, axis, route)


def halves(x):
    high = x.astype(jnp.bfloat16)
    low = (x - high.astype(jnp.float32)).astype(jnp.bfloat16)
    return high, low


def left_form(x):
    return jnp.concatenate(halves(x), axis=1)


def right_form(x):
    row = jnp.concatenate(halves(x), axis=1)
    return jnp.concatenate([row, row], axis=0)


def product(left, right):
    both = jnp.dot(left, right, preferred_element_type=jnp.float32)
    width = both.shape[1] // 2
    return both[:, :width] + both[:, width:]


def pick_kernel(side, send_hbm, p_ref, out_ref, send_ref, list_sem, sem):
    fetch = pltpu.make_async_copy(send_hbm, send_ref, list_sem)
    fetch.start()
    fetch.wait()
    for j in range(out_ref.shape[0]):
        row = jnp.maximum(send_ref[0, side, j], 0)
        pltpu.make_async_copy(p_ref.at[row], out_ref.at[j], sem).start()
    pltpu.make_async_copy(p_ref.at[pl.ds(0, out_ref.shape[0])], out_ref, sem).wait()


def local_kernel(col_ref, tile_ref, p_ref, a_ref, sum_ref, left_ref, link_ref, right_p, place_ref):
    blocks = p_ref.shape[0]
    neighbours = a_ref.shape[1]
    slots = left_ref.shape[0] - 1
    step = pl.program_id(0)

    @pl.when(step == 0)
    def _():
        @pl.loop(0, blocks)
        def _(f):
            right_p[f] = right_form(p_ref[f])

        @pl.loop(0, sum_ref.shape[0])
        def _(t):
            sum_ref[t] = jnp.zeros(sum_ref.shape[1:], jnp.float32)

        @pl.loop(0, slots + 1)
        def _(j):
            place_ref[j] = -1

    for i in range(STEP_BLOCKS):
        f = step * STEP_BLOCKS + i
        p_left = left_form(p_ref[f].T)
        for k in range(neighbours):
            v = col_ref[k, f]
            t = tile_ref[k, f]
            local = v < blocks
            slot = jnp.where(local, slots, v - blocks)
            left = product(p_left, right_form(a_ref[i, k]))
            left_cat = left_form(left)
            left_ref[slot] = left_cat
            place_ref[slot] = t
            triple = product(left_cat, right_p[jnp.minimum(v, blocks - 1)])
            sum_ref[t] += jnp.where(local, triple, 0.0)

    @pl.when(step == pl.num_programs(0) - 1)
    def _():
        @pl.loop(0, sum_ref.shape[0])
        def _(t):
            link_ref[slots + t] = slots

        @pl.loop(0, slots)
        def _(j):
            t = place_ref[j]
            link_ref[j] = slots

            @pl.when(t >= 0)
            def _():
                link_ref[j] = link_ref[slots + t]
                link_ref[slots + t] = j


def reduce_kernel(orders, link_hbm, part_ref, left_hbm, lower, upper, out_ref, link_ref, left, mine, chain, *rest):
    stages = len(orders[0])
    bufs = rest[:stages]
    load_sem, halo_sem, send_sem, recv_sem = rest[stages:]
    me = lax.axis_index("bulk")
    tiles = part_ref.shape[0]
    chunks = load_sem.shape[0]
    capacity = upper.shape[0]
    slots = 2 * capacity
    pieces = slots // PIECE
    width = tiles // chunks
    ways = len(orders)
    bit = [(me // 2**b) % 2 for b in range(stages)]
    partner = [me + 2**b * (1 - 2 * bit[b]) for b in range(stages)]

    def load(c, way):
        here = pl.ds(c * width, width)
        return pltpu.make_async_copy(part_ref.at[here], mine.at[here], load_sem.at[c])

    def keep(c, way, s):
        at = c * width
        size = width
        for level in range(s + 1):
            size //= 2
            at = at + bit[orders[way][level]] * size
        return at, size

    def scatter(c, way, s):
        b = orders[way][s]
        size = width >> (s + 1)
        if s == 0:
            src = mine.at[pl.ds(c * width + (1 - bit[b]) * size, size)]
        else:
            src = bufs[s - 1].at[c, pl.ds((1 - bit[b]) * size, size)]
        return pltpu.make_async_remote_copy(
            src_ref=src, dst_ref=bufs[s].at[c], send_sem=send_sem.at[s, c], recv_sem=recv_sem.at[s, c],
            device_id={"bulk": partner[b]}, device_id_type=pl.DeviceIdType.MESH)

    def gather(c, way, s):
        b = orders[way][s]
        at, size = keep(c, way, s)
        region = out_ref.at[pl.ds(at, size)]
        n = 2 * stages - 1 - s
        return pltpu.make_async_remote_copy(
            src_ref=region, dst_ref=region, send_sem=send_sem.at[n, c], recv_sem=recv_sem.at[n, c],
            device_id={"bulk": partner[b]}, device_id_type=pl.DeviceIdType.MESH)

    def add(c, way, s):
        b = orders[way][s]
        size = width >> (s + 1)
        at, _ = keep(c, way, s)

        def add_tile(j):
            if s == 0:
                own = mine[c * width + bit[b] * size + j]
            else:
                own = bufs[s - 1][c, bit[b] * size + j]
            total = bufs[s][c, j] + own
            if s == stages - 1:
                out_ref[at + j] = total
            else:
                bufs[s][c, j] = total

        if size % 2:
            pl.loop(0, size)(add_tile)
        else:
            @pl.loop(0, size // 2)
            def _(g):
                add_tile(2 * g)
                add_tile(2 * g + 1)

    def each(body):
        @pl.loop(0, chunks // ways)
        def _(g):
            for way in range(ways):
                body(g * ways + way, way)

    link_load = pltpu.make_async_copy(link_hbm, link_ref, halo_sem.at[pieces])

    def left_load(g):
        return pltpu.make_async_copy(
            left_hbm.at[pl.ds(g * PIECE, PIECE)], left.at[pl.ds(g * PIECE, PIECE)], halo_sem.at[g])

    link_load.start()
    for g in range(pieces):
        left_load(g).start()
    each(lambda c, way: load(c, way).start())
    barrier = pltpu.get_barrier_semaphore()
    for b in range(stages):
        pl.semaphore_signal(barrier, inc=1, device_id={"bulk": partner[b]}, device_id_type=pl.DeviceIdType.MESH)

    chain[slots] = jnp.zeros(chain.shape[1:], jnp.float32)
    link_load.wait()

    for side, arrived in enumerate((lower, upper)):
        @pl.loop(0, capacity // PIECE)
        def _(g, side=side, arrived=arrived):
            left_load(side * (capacity // PIECE) + g).wait()
            for i in range(PIECE):
                j = g * PIECE + i
                slot = side * capacity + j
                triple = product(left[slot], right_form(arrived[j]))
                chain[slot] = triple + chain[link_ref[slot]]

    pl.semaphore_wait(barrier, stages)

    def finish(c, way):
        load(c, way).wait()

        @pl.loop(0, width // 4)
        def _(g):
            for i in range(4):
                t = c * width + g * 4 + i
                mine[t] += chain[link_ref[slots + t]]
        scatter(c, way, 0).start()

    def reduce_step(c, way, s):
        scatter(c, way, s).wait_recv()
        add(c, way, s)
        if s + 1 < stages:
            scatter(c, way, s + 1).start()
        else:
            gather(c, way, s).start()

    for way in range(ways):
        finish(way, way)

    @pl.loop(1, chunks // ways)
    def _(g):
        for way in range(ways):
            finish(g * ways + way, way)
        for way in range(ways):
            reduce_step((g - 1) * ways + way, way, 0)

    for way in range(ways):
        reduce_step(chunks - ways + way, way, 0)
    for s in range(1, stages):
        each(functools.partial(reduce_step, s=s))
    for s in reversed(range(stages)):
        def spread_step(c, way, s=s):
            gather(c, way, s).wait_recv()
            if s > 0:
                gather(c, way, s - 1).start()
        each(spread_step)

    def drain(c, way):
        for s in range(stages):
            scatter(c, way, s).wait_send()
            gather(c, way, s).wait_send()
    each(drain)


def group_sum(links, partial, left, lower, upper):
    devices = lax.axis_size("bulk")
    stages = devices.bit_length() - 1
    tiles, rows, columns = partial.shape
    chunks = min(CHUNKS, tiles // devices)
    width = tiles // chunks
    capacity = upper.shape[0]
    bits = tuple(range(stages))
    if stages % 2:
        half = (stages - 1) // 2
        orders = (bits, bits[:1] + bits[1 + half:] + bits[1:1 + half])
    else:
        orders = (bits, bits[stages // 2:] + bits[:stages // 2])
    tile = (rows, columns)
    hbm_spec = pl.BlockSpec(memory_space=pltpu.HBM)
    vmem_spec = pl.BlockSpec(memory_space=pltpu.VMEM)
    vmem = functools.partial(pltpu.VMEM, dtype=jnp.float32)
    return pl.pallas_call(
        functools.partial(reduce_kernel, orders),
        out_shape=pltpu.VMEM(partial.shape, jnp.float32),
        in_specs=[hbm_spec] * 3 + [vmem_spec] * 2,
        out_specs=vmem_spec,
        scratch_shapes=[
            pltpu.SMEM(links.shape, jnp.int32),
            pltpu.VMEM((2 * capacity,) + left.shape[1:], left.dtype),
            vmem(partial.shape),
            vmem((2 * capacity + 1,) + tile),
        ]
        + [vmem((chunks, width >> (s + 1)) + tile) for s in range(stages)]
        + [
            pltpu.SemaphoreType.DMA((chunks,)),
            pltpu.SemaphoreType.DMA((2 * capacity // PIECE + 1,)),
            pltpu.SemaphoreType.DMA((2 * stages, chunks)),
            pltpu.SemaphoreType.DMA((2 * stages, chunks)),
        ],
        compiler_params=pltpu.CompilerParams(
            collective_id=0, has_side_effects=True, vmem_limit_bytes=SUM_VMEM_BYTES),
        cost_estimate=pl.CostEstimate(flops=tiles * rows * columns, bytes_accessed=8 * tiles * rows * columns, transcendentals=0),
        name="group_sum",
    )(links, partial, left, lower, upper)


def shards(p_tiles, a_tiles, col_ref, send_list, coarse_tile):
    blocks, rows, columns = p_tiles.shape
    neighbours = a_tiles.shape[1]
    capacity = send_list.shape[2]
    slots = 2 * capacity
    tile = (rows, columns)
    smem_spec = pl.BlockSpec(memory_space=pltpu.SMEM)
    vmem_spec = pl.BlockSpec(memory_space=pltpu.VMEM)
    hbm_spec = pl.BlockSpec(memory_space=pltpu.HBM)

    def picked(side, name):
        return pl.pallas_call(
            functools.partial(pick_kernel, side),
            out_shape=pltpu.VMEM((capacity,) + tile, jnp.float32),
            in_specs=[hbm_spec, hbm_spec],
            out_specs=vmem_spec,
            scratch_shapes=[pltpu.SMEM(send_list.shape, jnp.int32), pltpu.SemaphoreType.DMA, pltpu.SemaphoreType.DMA],
            compiler_params=pltpu.CompilerParams(vmem_limit_bytes=8 * 1024 * 1024),
            name=name,
        )(*(pltpu.with_memory_space_constraint(x, pltpu.HBM) for x in (send_list, p_tiles)))

    lower = shifted(picked(1, "pick_above"), ("group", "bulk"), 1)
    upper = shifted(picked(0, "pick_below"), ("group", "bulk"), -1)

    couplings = blocks * neighbours
    whole = lambda *shape: pl.BlockSpec(shape, lambda s, *_: (0,) * len(shape))
    partial, left, links = pl.pallas_call(
        local_kernel,
        out_shape=(
            jax.ShapeDtypeStruct((CT,) + tile, jnp.float32),
            jax.ShapeDtypeStruct((slots + 1, rows, 2 * columns), jnp.bfloat16),
            jax.ShapeDtypeStruct((-(-(slots + CT) // 128) * 128,), jnp.int32),
        ),
        grid_spec=pltpu.PrefetchScalarGridSpec(
            num_scalar_prefetch=2,
            grid=(blocks // STEP_BLOCKS,),
            in_specs=[
                whole(blocks, *tile),
                pl.BlockSpec((STEP_BLOCKS, neighbours) + tile, lambda s, *_: (s, 0, 0, 0)),
            ],
            out_specs=(whole(CT, *tile), whole(slots + 1, rows, 2 * columns), smem_spec),
            scratch_shapes=[pltpu.VMEM((blocks, 2 * rows, 2 * columns), jnp.bfloat16), pltpu.SMEM((slots + 1,), jnp.int32)],
        ),
        compiler_params=pltpu.CompilerParams(vmem_limit_bytes=VMEM_BYTES),
        cost_estimate=pl.CostEstimate(
            flops=couplings * 16 * rows * rows * columns, bytes_accessed=4 * couplings * rows * columns, transcendentals=0),
        name="local_products",
    )(col_ref.T, coarse_tile.T, p_tiles, a_tiles)

    lower, upper = (pltpu.with_memory_space_constraint(x, pltpu.VMEM) for x in (lower, upper))
    return group_sum(links, partial, left, lower, upper)


def solution(mesh):
    in_specs = (
        P(("group", "bulk"), None, None),
        P(("group", "bulk"), None, None, None),
        P(("group", "bulk"), None),
        P(("group", "bulk"), None, None),
        P(("group", "bulk"), None),
    )
    out_specs = P("group", None, None)
    return jax.shard_map(shards, mesh=mesh, in_specs=in_specs, out_specs=out_specs, check_vma=False)
```
